256 devices in a mesh: section: 16 (over y_lo, z), expert: 16 (over x, y_hi, core).
Axes of the slice: x: 4, y: 4 (y_hi: 2, y_lo: 2; y = y_hi * 2 + y_lo), z: 8, core: 2. Of those that a mesh axis runs over, the one named last changes fastest.
Arguments:
- activations: bfloat16 [16, 2048, 2048], P('section', 'expert'), may hold values from -6 to 6
- norm_gain: float32 [16, 2048], P('section'), may hold values from 0.1 to 1.9
- w_gate: bfloat16 [16, 2048, 11264], P('section', None, 'expert'), may hold values from -0.125 to 0.125
- w_up: bfloat16 [16, 2048, 11264], P('section', None, 'expert'), may hold values from -0.125 to 0.125
- w_down: bfloat16 [16, 11264, 2048], P('section', 'expert'), may hold values from -0.15625 to 0.15625
- routes: int32 [2, 16, 2048, 2], P(None, 'section', 'expert'), may hold values from 0 to 7, all different within a row; in each aligned block of 128 rows (0 to 127, 128 to 255, ..., all dimensions but the last counted through in order) at most 48 rows name the same one
- gate_levels: int32 [2, 16, 2048, 2], P(None, 'section', 'expert'), may hold values from 1 to 8
Outputs:
- passed_on: bfloat16 [16, 2048, 2048], P('section', 'expert')
The draws below stay inside these ranges and needn't reach their ends.
Inputs may be any that keep to these rules, and one draw needn't show every extreme that they name: `routes`: the 2 experts of a token differ. Among the 128 tokens of one index of expert in one stop and section, no expert is named by more than 48 tokens, and in every draw some expert is named by exactly 48 of them.
All inputs are finite; a program needn't handle non-finite values.
Results may differ from the reference program's by a relative error of at most 0.0065.
Values may be sent and summed in bfloat16 or wider, within the bound.
No kernel may reach another device: no remote copies, remote signals or barrier semaphores. Data moves between devices by JAX's collectives and lax.ppermute only.
A program may use at most 64 MiB of HBM per device.

```python
import math
import jax
import jax.numpy as jnp
import numpy as np
from jax import lax

D = 2048
FF = 1408
TOK_DEV = 128
TOP = 2
STOPS = 2
LAYERS = 16
EXPERTS = 8
CAP = 48
MB = 2048
N_EXPERT = 16


def set_ends(result, key, smallest, top_value):
    extent = result.shape
    spot = [jax.random.randint(jax.random.fold_in(key, axis), (), 0, extent[axis]) for axis in range(len(extent))]
    result = result.at[tuple(spot)].set(smallest)
    longest = extent.index(max(extent))
    spot[longest] = (spot[longest] + 1) % extent[longest]
    return result.at[tuple(spot)].set(top_value)


def block_scale(key, dims, split, least, top_value):
    factor_of = 1.0
    for dim, blocks in split:
        draws = jax.random.uniform(jax.random.fold_in(jax.random.fold_in(key, 6), dim), (blocks,), jnp.float32, least / len(split), top_value / len(split))
        factor_of = factor_of * jnp.repeat(jnp.exp(draws), dims[dim] // blocks).reshape((-1,) + (1,) * (len(dims) - 1 - dim))
    return factor_of


def assign_block(own_key, own, number, rows, amount, top, limit, lean):
    sequence = jax.random.permutation(own_key, amount)
    crowded, common = portions_of(amount, rows * top, limit, lean, True), portions_of(amount, rows * top, limit, lean, False)
    places = jnp.arange(amount)

    def named(tallies, offset_by):
        used = int((tallies > 0).sum())
        fixed = max(1, used // 4)
        passed = fixed + (places - fixed + offset_by * (used - fixed)) % max(1, amount - fixed)
        return jnp.zeros((amount,), jnp.int32).at[sequence[jnp.where(places < fixed, places, passed)]].set(jnp.asarray(tallies, jnp.int32))

    tallies = jnp.where(number % 4 == 0, named(crowded, number // 4), named(common, number - number // 4 - 1))
    mixed = jax.random.permutation(jax.random.fold_in(own, 3), amount)
    source_of, sink = mixed[0:amount // 2 * 2:2], mixed[1:amount // 2 * 2:2]
    slack = jnp.minimum(tallies[source_of] - 1, limit - tallies[sink]) // 2
    slack = jnp.where((source_of == sequence[0]) | (sink == sequence[0]) | (tallies[sink] == 0), 0, jnp.maximum(slack, 0))
    passed = jax.random.randint(jax.random.fold_in(own, 4), (amount // 2,), 0, 1 << 20) % (slack + 1)
    tallies = tallies.at[source_of].add(-passed).at[sink].add(passed)
    labels = jnp.searchsorted(jnp.cumsum(tallies), jnp.arange(rows * top), side="right").astype(jnp.int32)
    table = labels.reshape(top, rows).T
    table = table[jax.random.permutation(jax.random.fold_in(own, 1), rows)]
    offset_by = jax.random.randint(jax.random.fold_in(own, 2), (rows, 1), 0, top)
    return jnp.take_along_axis(table, (jnp.arange(top)[None, :] + offset_by) % top, axis=1)


def portions_of(count, total, bound, lean, full):
    weights = [(1 << 20) // math.isqrt(rank ** lean) + 1 for rank in range(1, count + 1)]
    largest = bound if full else min(bound, max(-(-total // count), total * weights[0] // sum(weights)))
    least = 1 if total - largest >= count - 1 else 0
    given, surplus = [largest] + [least] * (count - 1), total - largest - least * (count - 1)
    while surplus > 0:
        movable = [i for i in range(1, count) if given[i] < largest] or [i for i in range(1, count) if given[i] < bound]
        mass, budget = sum([weights[i] for i in movable]), surplus
        for i in movable:
            more = min(bound - given[i], max(1, budget * weights[i] // mass), surplus)
            given[i] = given[i] + more
            surplus = surplus - more
    return np.array(given)


def normal_values(key, extent, width, most, cuts=(), kind=jnp.bfloat16):
    entries = width * jax.random.normal(key, extent, jnp.float32)
    if cuts:
        entries = entries * block_scale(key, extent, cuts, -0.22, 0.18)
    return jnp.clip(entries, -most, most).astype(kind)


def setup_inputs(seed: int = 0) -> dict:
    arg_keys = jax.random.split(jax.random.key(seed), 8)
    activations = normal_values(arg_keys[0], (LAYERS, MB, D), 1.0, 6.0, ((0, 16), (1, 16)))
    norm_gain = jnp.clip(1.0 + 0.18 * jax.random.normal(arg_keys[1], (LAYERS, D), jnp.float32), 0.1, 1.9)
    w_gate = normal_values(arg_keys[2], (LAYERS, D, EXPERTS * FF), D ** -0.5, 0.125, ((0, 16), (2, 16)))
    w_up = normal_values(arg_keys[3], (LAYERS, D, EXPERTS * FF), D ** -0.5, 0.125, ((0, 16), (2, 16)))
    w_down = normal_values(arg_keys[4], (LAYERS, EXPERTS * FF, D), FF ** -0.5, 0.15625, ((0, 16), (1, 16)))
    routes_keys = jax.random.split(jax.random.fold_in(arg_keys[5], 1), STOPS * LAYERS * MB // TOK_DEV)
    routes_turns = jax.random.permutation(jax.random.fold_in(arg_keys[5], 3), STOPS * LAYERS * MB // TOK_DEV)
    routes = jax.vmap(lambda own, number: assign_block(jax.random.fold_in(arg_keys[5], 2), own, number, TOK_DEV, EXPERTS, TOP, CAP, 2))(routes_keys, routes_turns).reshape((STOPS, LAYERS, MB, TOP))
    gate_levels = set_ends(jax.random.randint(arg_keys[6], (STOPS, LAYERS, MB, TOP), 1, 9), jax.random.fold_in(arg_keys[6], 1), 1, 8).astype(jnp.int32)
    return {"activations": activations, "norm_gain": norm_gain, "w_gate": w_gate, "w_up": w_up, "w_down": w_down, "routes": routes, "gate_levels": gate_levels}


def slot_positions(route_rows, experts):
    onehot = (route_rows[:, :, None] == jnp.arange(experts, dtype=jnp.int32)[None, None, :]).astype(jnp.int32)
    present = lax.optimization_barrier(jnp.sum(onehot, axis=1))
    before = jnp.cumsum(present, axis=0) - present
    return lax.optimization_barrier(jnp.sum(onehot * before[:, None, :], axis=2)).astype(jnp.int32)

def one_section(stream, gain, gate_cols, up_cols, down_rows, route_rows, levels):
    streamf = stream.astype(jnp.float32)
    variance = lax.optimization_barrier(jnp.mean(streamf * streamf, axis=-1, keepdims=True))
    normed = (streamf * lax.rsqrt(variance + 1e-06) * gain).astype(jnp.bfloat16)
    levelf = levels.astype(jnp.float32)
    weights = levelf / lax.optimization_barrier(jnp.sum(levelf, axis=-1, keepdims=True))
    routed = route_rows.reshape(N_EXPERT, TOK_DEV, TOP)
    slots = jax.vmap(lambda rows: slot_positions(rows, EXPERTS))(routed)
    source = jnp.broadcast_to(jnp.arange(N_EXPERT, dtype=jnp.int32)[:, None, None], routed.shape)
    normed_rows = jnp.broadcast_to(normed.reshape(N_EXPERT, TOK_DEV, 1, D), (N_EXPERT, TOK_DEV, TOP, D))
    buffer = jnp.zeros((EXPERTS, N_EXPERT, CAP, D), normed.dtype).at[routed, source, slots].set(normed_rows)
    gate_each = jnp.moveaxis(gate_cols.reshape(D, EXPERTS, FF), 1, 0)
    up_each = jnp.moveaxis(up_cols.reshape(D, EXPERTS, FF), 1, 0)
    down_each = down_rows.reshape(EXPERTS, FF, D)

    def one_expert(items):
        rows, gate_w, up_w, down_w = items
        flat = rows.reshape(N_EXPERT * CAP, D)
        gate = jnp.dot(flat, gate_w, preferred_element_type=jnp.float32)
        up = jnp.dot(flat, up_w, preferred_element_type=jnp.float32)
        hidden = (jax.nn.silu(gate) * up).astype(jnp.bfloat16)
        out = jnp.dot(hidden, down_w, preferred_element_type=jnp.float32).astype(jnp.bfloat16)
        return out.reshape(N_EXPERT, CAP, D)
    expert_out = lax.map(one_expert, (buffer, gate_each, up_each, down_each))
    picked = expert_out[routed, source, slots].astype(jnp.float32)
    branch = lax.optimization_barrier(jnp.sum(weights.reshape(N_EXPERT, TOK_DEV, TOP)[..., None] * picked, axis=2))
    updated = (streamf + branch.reshape(MB, D)).astype(jnp.bfloat16)
    return updated

def reference(activations, norm_gain, w_gate, w_up, w_down, routes, gate_levels):
    stream = activations
    for stop_index in range(STOPS):

        def per_section(items):
            return one_section(*items)
        updated = lax.map(per_section, (stream, norm_gain, w_gate, w_up, w_down, routes[stop_index], gate_levels[stop_index]))
        stream = jnp.roll(updated, 1, axis=0)
    return stream
```

```python
import functools

import jax
import jax.numpy as jnp
from jax import lax
from jax.experimental import pallas as pl
from jax.experimental.pallas import tpu as pltpu
from jax.sharding import PartitionSpec as P

STOPS = 2
CAPACITY = 48
EPS = 1e-06
CHUNKS = 1
DEPTH = 2
MIB = 1024 * 1024
VMEM = pl.BlockSpec(memory_space=pltpu.VMEM)


def passed_along(value, axis, by):
    devices = lax.axis_size(axis)
    return lax.ppermute(value, axis, [(i, (i + by) % devices) for i in range(devices)])


def sibling(value):
    devices = lax.axis_size("expert")
    return lax.ppermute(value, "expert", [(i, i ^ 1) for i in range(devices)])


def across_chips(value, experts):
    groups = [[2 * chip + core for chip in range(experts)] for core in range(2)]
    shape = (experts, value.shape[0] // experts, value.shape[1])
    moved = lax.all_to_all(
        value.reshape(shape),
        "expert",
        split_axis=0,
        concat_axis=0,
        axis_index_groups=groups,
        tiled=True,
    )
    return moved.reshape(value.shape)


def product(a, b):
    return jnp.dot(a, b, preferred_element_type=jnp.float32)


def product_t(a, b):
    return lax.dot_general(a, b, (((1,), (1,)), ((), ())), preferred_element_type=jnp.float32)


def slot_of_token(routes, experts):
    tokens = routes.shape[1]
    expert_ids = lax.broadcasted_iota(jnp.int32, (experts, tokens), 0)
    named = [routes[k : k + 1, :] == expert_ids for k in range(routes.shape[0])]
    present = functools.reduce(jnp.logical_or, named)
    earlier = lax.broadcasted_iota(jnp.int32, (tokens, tokens), 0) < lax.broadcasted_iota(
        jnp.int32, (tokens, tokens), 1
    )
    ones = jnp.where(present, 1.0, 0.0)
    before = product(ones.astype(jnp.bfloat16), jnp.where(earlier, 1.0, 0.0).astype(jnp.bfloat16))
    before = jnp.where(present, before, -1.0).astype(jnp.int32)
    slot_ids = lax.broadcasted_iota(jnp.int32, (experts, CAPACITY, tokens), 1)
    return named, before[:, None, :] == slot_ids


def dispatch_kernel(stop, routes_ref, stream_ref, rows_ref):
    experts = rows_ref.shape[0] // CAPACITY
    _, hit = slot_of_token(routes_ref[stop], experts)
    chosen = jnp.where(hit, 1.0, 0.0).reshape(rows_ref.shape[0], -1).astype(jnp.bfloat16)
    width = rows_ref.shape[1]
    step = 512
    for n in range(0, width, step):
        cols = slice(n, n + step)
        rows_ref[:, cols] = product(chosen, stream_ref[:, cols]).astype(jnp.bfloat16)


def combine_kernel(stop, routes_ref, levels_ref, back_ref, stream_ref, out_ref):
    slots = back_ref.shape[0]
    experts = slots // CAPACITY
    named, hit = slot_of_token(routes_ref[stop], experts)
    levels = levels_ref[stop].astype(jnp.float32)
    level = sum(jnp.where(at, levels[k : k + 1, :], 0.0) for k, at in enumerate(named))
    leveled = jnp.where(hit, level[:, None, :], 0.0).reshape(slots, -1).T
    total = jnp.sum(leveled, axis=1, keepdims=True)
    leveled = leveled.astype(jnp.bfloat16)
    width = out_ref.shape[1]
    step = 512
    for n in range(0, width, step):
        cols = slice(n, n + step)
        branch = product(leveled, back_ref[:, cols]) / total
        out_ref[:, cols] = (stream_ref[:, cols].astype(jnp.float32) + branch).astype(jnp.bfloat16)


def dispatch(stop, routes, stream, experts):
    tokens, width = stream.shape
    count = experts * CAPACITY
    return pl.pallas_call(
        functools.partial(dispatch_kernel, stop),
        out_shape=jax.ShapeDtypeStruct((count, width), stream.dtype),
        in_specs=[VMEM] * 2,
        out_specs=VMEM,
        compiler_params=pltpu.CompilerParams(vmem_limit_bytes=24 * MIB),
        cost_estimate=pl.CostEstimate(
            flops=2 * count * tokens * width,
            bytes_accessed=2 * (count + tokens) * width,
            transcendentals=0,
        ),
        name="dispatch",
    )(routes, stream)


def combine(stop, routes, levels, back, stream):
    tokens, width = stream.shape
    count = back.shape[0]
    return pl.pallas_call(
        functools.partial(combine_kernel, stop),
        out_shape=jax.ShapeDtypeStruct((tokens, width), stream.dtype),
        in_specs=[VMEM] * 4,
        out_specs=VMEM,
        compiler_params=pltpu.CompilerParams(vmem_limit_bytes=24 * MIB),
        cost_estimate=pl.CostEstimate(
            flops=2 * count * tokens * width,
            bytes_accessed=2 * (count + 2 * tokens) * width,
            transcendentals=0,
        ),
        name="combine",
    )(routes, levels, back, stream)


FIRST = 256


def expert_kernel(*refs):
    parts, (gain_ref, gate0, up0, gate1, up1, down0, down1) = refs[:CHUNKS], refs[CHUNKS : CHUNKS + 7]
    out_ref, hidden_ref = refs[CHUNKS + 7 : CHUNKS + 9]
    gates, ups, downs, normed_ref, sems = refs[CHUNKS + 9 :]
    half, width = gate0.shape
    cut = out_ref.shape[1]
    head, tail = pl.ds(0, FIRST), pl.ds(FIRST, half - FIRST)
    every, cols = pl.ds(0, half), pl.ds(0, cut)
    blocks = [
        [(gate0.at[head], gates.at[0, head]), (up0.at[head], ups.at[0, head])],
        [(gate0.at[tail], gates.at[0, tail]), (up0.at[tail], ups.at[0, tail])],
        [(gate1, gates.at[1]), (up1, ups.at[1])],
        [(down0.at[every, cols], downs.at[0]), (down1.at[every, cols], downs.at[1])],
    ]
    copies = [
        [pltpu.make_async_copy(src, dst, sems.at[b, i]) for i, (src, dst) in enumerate(block)]
        for b, block in enumerate(blocks)
    ]

    def fetch(b):
        for copy in copies[b]:
            copy.start()

    def arrive(b):
        for copy in copies[b]:
            copy.wait()
        if b + DEPTH < len(copies):
            fetch(b + DEPTH)

    for b in range(DEPTH):
        fetch(b)
    rowsf = [part[...].astype(jnp.float32) for part in parts]
    variance = sum(jnp.sum(x * x, axis=-1, keepdims=True) for x in rowsf) / width
    scale = lax.rsqrt(variance + EPS)
    for c, x in enumerate(rowsf):
        at = slice(c * cut, (c + 1) * cut)
        normed_ref[:, at] = (x * scale * gain_ref[:, at]).astype(jnp.bfloat16)

    def hide(side, begin, end):
        gate = product_t(normed_ref[...], gates[side, begin:end])
        up = product_t(normed_ref[...], ups[side, begin:end])
        hidden_ref[side, :, begin:end] = (gate / (1.0 + jnp.exp(-gate)) * up).astype(jnp.bfloat16)

    arrive(0)
    hide(0, 0, FIRST)
    arrive(1)
    hide(0, FIRST, half)
    arrive(2)
    hide(1, 0, half)
    arrive(3)
    down_part(hidden_ref, downs, out_ref)


def down_part(hidden_ref, downs, out_ref):
    for n in range(0, out_ref.shape[1], 512):
        at = slice(n, n + 512)
        out = product(hidden_ref[0], downs[0, :, at]) + product(hidden_ref[1], downs[1, :, at])
        out_ref[:, at] = out.astype(jnp.bfloat16)


def later_kernel(chunk, hidden_ref, down0, down1, out_ref, downs, sems):
    half, cut = downs.shape[1:]
    cols = pl.ds(chunk * cut, cut)
    copies = [
        pltpu.make_async_copy(down.at[pl.ds(0, half), cols], downs.at[i], sems.at[i])
        for i, down in enumerate((down0, down1))
    ]
    for copy in copies:
        copy.start()
    for copy in copies:
        copy.wait()
    down_part(hidden_ref, downs, out_ref)


def expert(parts, gain, gates, ups, downs):
    count, cut = parts[0].shape
    half, width = gates[0].shape
    stored = pl.BlockSpec(memory_space=pl.ANY)
    out, hidden = pl.pallas_call(
        expert_kernel,
        out_shape=[
            jax.ShapeDtypeStruct((count, cut), jnp.bfloat16),
            jax.ShapeDtypeStruct((2, count, half), jnp.bfloat16),
        ],
        in_specs=[VMEM] * (CHUNKS + 1) + [stored] * 6,
        out_specs=[VMEM] * 2,
        scratch_shapes=[
            pltpu.VMEM((2, half, width), jnp.bfloat16),
            pltpu.VMEM((2, half, width), jnp.bfloat16),
            pltpu.VMEM((2, half, cut), jnp.bfloat16),
            pltpu.VMEM((count, width), jnp.bfloat16),
            pltpu.SemaphoreType.DMA((4, 2)),
        ],
        compiler_params=pltpu.CompilerParams(vmem_limit_bytes=56 * MIB),
        cost_estimate=pl.CostEstimate(
            flops=8 * count * width * half + 4 * count * cut * half,
            bytes_accessed=8 * half * width + 4 * half * cut + 4 * count * width,
            transcendentals=2 * count * half,
        ),
        name="expert",
    )(*parts, gain, gates[0], ups[0], gates[1], ups[1], *downs)
    outs = [out]
    for chunk in range(1, CHUNKS):
        outs.append(
            pl.pallas_call(
                functools.partial(later_kernel, chunk),
                out_shape=jax.ShapeDtypeStruct((count, cut), jnp.bfloat16),
                in_specs=[VMEM] + [stored] * 2,
                out_specs=VMEM,
                scratch_shapes=[
                    pltpu.VMEM((2, half, cut), jnp.bfloat16),
                    pltpu.SemaphoreType.DMA((2,)),
                ],
                compiler_params=pltpu.CompilerParams(vmem_limit_bytes=56 * MIB),
                cost_estimate=pl.CostEstimate(
                    flops=4 * count * cut * half,
                    bytes_accessed=4 * half * cut + 2 * count * cut,
                    transcendentals=0,
                ),
                name="later",
            )(hidden, *downs)
        )
    return outs


def on_device(activations, norm_gain, w_gate, w_up, w_down, routes, gate_levels):
    experts = lax.axis_size("expert") // 2
    cut = activations.shape[2] // CHUNKS
    by_token = routes[:, 0].transpose(0, 2, 1)
    levels = gate_levels[:, 0].transpose(0, 2, 1)
    stream = [activations[0, :, c * cut : (c + 1) * cut] for c in range(CHUNKS)]
    gates, ups, downs = [[w[0].T] for w in (w_gate, w_up)] + [[w_down[0]]]
    for s in range(STOPS):
        parts = [across_chips(dispatch(s, by_token, part, experts), experts) for part in stream]
        if s == 0:
            for halves in (gates, ups, downs):
                halves.append(sibling(halves[0]))
        outs = expert(parts, norm_gain, gates, ups, downs)
        stream = [
            passed_along(
                combine(s, by_token, levels, across_chips(out, experts), part), "section", 1
            )
            for out, part in zip(outs, stream)
        ]
    return jnp.concatenate(stream, axis=1)[None]


def solution(mesh):
    in_specs = (
        P("section", "expert", None),
        P("section", None),
        P("section", None, "expert"),
        P("section", None, "expert"),
        P("section", "expert", None),
        P(None, "section", "expert", None),
        P(None, "section", "expert", None),
    )
    out_specs = P("section", "expert", None)
    return jax.shard_map(
        on_device, mesh=mesh, in_specs=in_specs, out_specs=out_specs, check_vma=False
    )
```

```python
import functools

import jax
import jax.numpy as jnp
from jax import lax
from jax.experimental import pallas as pl
from jax.experimental.pallas import tpu as pltpu
from jax.sharding import PartitionSpec as P

STOPS = 2
CAPACITY = 48
EPS = 1e-06
DEPTH = 2
MIB = 1024 * 1024
VMEM = pl.BlockSpec(memory_space=pltpu.VMEM)


def passed_along(value, axis, by):
    devices = lax.axis_size(axis)
    return lax.ppermute(value, axis, [(i, (i + by) % devices) for i in range(devices)])


def sibling(value):
    devices = lax.axis_size("expert")
    return lax.ppermute(value, "expert", [(i, i ^ 1) for i in range(devices)])


def across_chips(value, experts):
    groups = [[2 * chip + core for chip in range(experts)] for core in range(2)]
    shape = (experts, value.shape[0] // experts, value.shape[1])
    moved = lax.all_to_all(
        value.reshape(shape),
        "expert",
        split_axis=0,
        concat_axis=0,
        axis_index_groups=groups,
        tiled=True,
    )
    return moved.reshape(value.shape)


def product(a, b):
    return jnp.dot(a, b, preferred_element_type=jnp.float32)


def product_t(a, b):
    return lax.dot_general(a, b, (((1,), (1,)), ((), ())), preferred_element_type=jnp.float32)


def slot_of_token(routes, experts):
    tokens = routes.shape[1]
    expert_ids = lax.broadcasted_iota(jnp.int32, (experts, tokens), 0)
    named = [routes[k : k + 1, :] == expert_ids for k in range(routes.shape[0])]
    present = functools.reduce(jnp.logical_or, named)
    earlier = lax.broadcasted_iota(jnp.int32, (tokens, tokens), 0) < lax.broadcasted_iota(
        jnp.int32, (tokens, tokens), 1
    )
    ones = jnp.where(present, 1.0, 0.0)
    before = product(ones.astype(jnp.bfloat16), jnp.where(earlier, 1.0, 0.0).astype(jnp.bfloat16))
    before = jnp.where(present, before, -1.0).astype(jnp.int32)
    slot_ids = lax.broadcasted_iota(jnp.int32, (experts, CAPACITY, tokens), 1)
    return named, before[:, None, :] == slot_ids


def dispatch_kernel(stop, routes_ref, stream_ref, rows_ref):
    experts = rows_ref.shape[0] // CAPACITY
    _, hit = slot_of_token(routes_ref[stop], experts)
    chosen = jnp.where(hit, 1.0, 0.0).reshape(rows_ref.shape[0], -1).astype(jnp.bfloat16)
    width = rows_ref.shape[1]
    step = 512
    for n in range(0, width, step):
        cols = slice(n, n + step)
        rows_ref[:, cols] = product(chosen, stream_ref[:, cols]).astype(jnp.bfloat16)


def combine_kernel(stop, routes_ref, levels_ref, back_ref, stream_ref, out_ref):
    slots = back_ref.shape[0]
    experts = slots // CAPACITY
    named, hit = slot_of_token(routes_ref[stop], experts)
    levels = levels_ref[stop].astype(jnp.float32)
    level = sum(jnp.where(at, levels[k : k + 1, :], 0.0) for k, at in enumerate(named))
    leveled = jnp.where(hit, level[:, None, :], 0.0).reshape(slots, -1).T
    total = jnp.sum(leveled, axis=1, keepdims=True)
    leveled = leveled.astype(jnp.bfloat16)
    width = out_ref.shape[1]
    step = 512
    for n in range(0, width, step):
        cols = slice(n, n + step)
        branch = product(leveled, back_ref[:, cols]) / total
        out_ref[:, cols] = (stream_ref[:, cols].astype(jnp.float32) + branch).astype(jnp.bfloat16)


def dispatch(stop, routes, stream, experts):
    tokens, width = stream.shape
    count = experts * CAPACITY
    return pl.pallas_call(
        functools.partial(dispatch_kernel, stop),
        out_shape=jax.ShapeDtypeStruct((count, width), stream.dtype),
        in_specs=[VMEM] * 2,
        out_specs=VMEM,
        compiler_params=pltpu.CompilerParams(vmem_limit_bytes=24 * MIB),
        cost_estimate=pl.CostEstimate(
            flops=2 * count * tokens * width,
            bytes_accessed=2 * (count + tokens) * width,
            transcendentals=0,
        ),
        name="dispatch",
    )(routes, stream)


def combine(stop, routes, levels, back, stream):
    tokens, width = stream.shape
    count = back.shape[0]
    return pl.pallas_call(
        functools.partial(combine_kernel, stop),
        out_shape=jax.ShapeDtypeStruct((tokens, width), stream.dtype),
        in_specs=[VMEM] * 4,
        out_specs=VMEM,
        compiler_params=pltpu.CompilerParams(vmem_limit_bytes=24 * MIB),
        cost_estimate=pl.CostEstimate(
            flops=2 * count * tokens * width,
            bytes_accessed=2 * (count + 2 * tokens) * width,
            transcendentals=0,
        ),
        name="combine",
    )(routes, levels, back, stream)


FIRST = 256


def expert_kernel(rows_ref, gain_ref, *refs):
    gate0, up0, gate1, up1, down0, down1, out_ref = refs[:7]
    gates, ups, downs, normed_ref, hidden_ref, sems = refs[7:]
    half = gate0.shape[0]
    head, tail = pl.ds(0, FIRST), pl.ds(FIRST, half - FIRST)
    blocks = [
        [(gate0.at[head], gates.at[0, head]), (up0.at[head], ups.at[0, head])],
        [(gate0.at[tail], gates.at[0, tail]), (up0.at[tail], ups.at[0, tail])],
        [(gate1, gates.at[1]), (up1, ups.at[1])],
        [(down0, downs.at[0]), (down1, downs.at[1])],
    ]
    copies = [
        [pltpu.make_async_copy(src, dst, sems.at[b, i]) for i, (src, dst) in enumerate(block)]
        for b, block in enumerate(blocks)
    ]

    def fetch(b):
        for copy in copies[b]:
            copy.start()

    def arrive(b):
        for copy in copies[b]:
            copy.wait()
        if b + DEPTH < len(copies):
            fetch(b + DEPTH)

    def hide(side, begin, end):
        gate = product_t(normed_ref[...], gates[side, begin:end])
        up = product_t(normed_ref[...], ups[side, begin:end])
        hidden_ref[side, :, begin:end] = (gate / (1.0 + jnp.exp(-gate)) * up).astype(jnp.bfloat16)

    for b in range(DEPTH):
        fetch(b)
    rowsf = rows_ref[...].astype(jnp.float32)
    variance = jnp.mean(rowsf * rowsf, axis=-1, keepdims=True)
    normed_ref[...] = (rowsf * lax.rsqrt(variance + EPS) * gain_ref[...]).astype(jnp.bfloat16)
    arrive(0)
    hide(0, 0, FIRST)
    arrive(1)
    hide(0, FIRST, half)
    arrive(2)
    hide(1, 0, half)
    arrive(3)
    for n in range(0, out_ref.shape[1], 512):
        at = slice(n, n + 512)
        out = product(hidden_ref[0], downs[0, :, at]) + product(hidden_ref[1], downs[1, :, at])
        out_ref[:, at] = out.astype(jnp.bfloat16)


def expert(rows, gain, gates, ups, downs):
    count, width = rows.shape
    half = gates[0].shape[0]
    block = pltpu.VMEM((2, half, width), jnp.bfloat16)
    return pl.pallas_call(
        expert_kernel,
        out_shape=jax.ShapeDtypeStruct((count, width), jnp.bfloat16),
        in_specs=[VMEM] * 2 + [pl.BlockSpec(memory_space=pl.ANY)] * 6,
        out_specs=VMEM,
        scratch_shapes=[block] * 3
        + [
            pltpu.VMEM((count, width), jnp.bfloat16),
            pltpu.VMEM((2, count, half), jnp.bfloat16),
            pltpu.SemaphoreType.DMA((4, 2)),
        ],
        compiler_params=pltpu.CompilerParams(vmem_limit_bytes=59 * MIB),
        cost_estimate=pl.CostEstimate(
            flops=12 * count * width * half,
            bytes_accessed=12 * half * width + 4 * count * width,
            transcendentals=2 * count * half,
        ),
        name="expert",
    )(rows, gain, gates[0], ups[0], gates[1], ups[1], *downs)


def on_device(activations, norm_gain, w_gate, w_up, w_down, routes, gate_levels):
    experts = lax.axis_size("expert") // 2
    by_token = routes[:, 0].transpose(0, 2, 1)
    levels = gate_levels[:, 0].transpose(0, 2, 1)
    stream = activations[0]
    gates, ups, downs = [[w, sibling(w)] for w in (w_gate[0].T, w_up[0].T, w_down[0])]
    for s in range(STOPS):
        rows = across_chips(dispatch(s, by_token, stream, experts), experts)
        back = across_chips(expert(rows, norm_gain, gates, ups, downs), experts)
        stream = passed_along(combine(s, by_token, levels, back, stream), "section", 1)
    return stream[None]


def solution(mesh):
    in_specs = (
        P("section", "expert", None),
        P("section", None),
        P("section", None, "expert"),
        P("section", None, "expert"),
        P("section", "expert", None),
        P(None, "section", "expert", None),
        P(None, "section", "expert", None),
    )
    out_specs = P("section", "expert", None)
    return jax.shard_map(
        on_device, mesh=mesh, in_specs=in_specs, out_specs=out_specs, check_vma=False
    )
```

```python
import functools

import jax
import jax.numpy as jnp
from jax import lax
from jax.experimental import pallas as pl
from jax.experimental.pallas import tpu as pltpu
from jax.sharding import PartitionSpec as P

STOPS = 2
CAPACITY = 48
EPS = 1e-06
DEPTH = 2
MIB = 1024 * 1024
VMEM = pl.BlockSpec(memory_space=pltpu.VMEM)


def passed_along(value, axis, by):
    devices = lax.axis_size(axis)
    return lax.ppermute(value, axis, [(i, (i + by) % devices) for i in range(devices)])


def sibling(value):
    devices = lax.axis_size("expert")
    return lax.ppermute(value, "expert", [(i, i ^ 1) for i in range(devices)])


def across_chips(value, experts):
    groups = [[2 * chip + core for chip in range(experts)] for core in range(2)]
    shape = (experts, value.shape[0] // experts, value.shape[1])
    moved = lax.all_to_all(
        value.reshape(shape),
        "expert",
        split_axis=0,
        concat_axis=0,
        axis_index_groups=groups,
        tiled=True,
    )
    return moved.reshape(value.shape)


def product(a, b):
    return jnp.dot(a, b, preferred_element_type=jnp.float32)


def product_t(a, b):
    return lax.dot_general(a, b, (((1,), (1,)), ((), ())), preferred_element_type=jnp.float32)


def slot_of_token(routes, experts):
    tokens = routes.shape[1]
    expert_ids = lax.broadcasted_iota(jnp.int32, (experts, tokens), 0)
    named = [routes[k : k + 1, :] == expert_ids for k in range(routes.shape[0])]
    present = functools.reduce(jnp.logical_or, named)
    earlier = lax.broadcasted_iota(jnp.int32, (tokens, tokens), 0) < lax.broadcasted_iota(
        jnp.int32, (tokens, tokens), 1
    )
    ones = jnp.where(present, 1.0, 0.0)
    before = product(ones.astype(jnp.bfloat16), jnp.where(earlier, 1.0, 0.0).astype(jnp.bfloat16))
    before = jnp.where(present, before, -1.0).astype(jnp.int32)
    slot_ids = lax.broadcasted_iota(jnp.int32, (experts, CAPACITY, tokens), 1)
    return named, before[:, None, :] == slot_ids


def dispatch_kernel(stop, routes_ref, stream_ref, rows_ref):
    experts = rows_ref.shape[0] // CAPACITY
    _, hit = slot_of_token(routes_ref[stop], experts)
    chosen = jnp.where(hit, 1.0, 0.0).reshape(rows_ref.shape[0], -1).astype(jnp.bfloat16)
    width = rows_ref.shape[1]
    step = 512
    for n in range(0, width, step):
        cols = slice(n, n + step)
        rows_ref[:, cols] = product(chosen, stream_ref[:, cols]).astype(jnp.bfloat16)


def combine_kernel(stop, routes_ref, levels_ref, back_ref, stream_ref, out_ref):
    slots = back_ref.shape[0]
    experts = slots // CAPACITY
    named, hit = slot_of_token(routes_ref[stop], experts)
    levels = levels_ref[stop].astype(jnp.float32)
    level = sum(jnp.where(at, levels[k : k + 1, :], 0.0) for k, at in enumerate(named))
    leveled = jnp.where(hit, level[:, None, :], 0.0).reshape(slots, -1).T
    total = jnp.sum(leveled, axis=1, keepdims=True)
    leveled = leveled.astype(jnp.bfloat16)
    width = out_ref.shape[1]
    step = 512
    for n in range(0, width, step):
        cols = slice(n, n + step)
        branch = product(leveled, back_ref[:, cols]) / total
        out_ref[:, cols] = (stream_ref[:, cols].astype(jnp.float32) + branch).astype(jnp.bfloat16)


def dispatch(stop, routes, stream, experts):
    tokens, width = stream.shape
    count = experts * CAPACITY
    return pl.pallas_call(
        functools.partial(dispatch_kernel, stop),
        out_shape=jax.ShapeDtypeStruct((count, width), stream.dtype),
        in_specs=[VMEM] * 2,
        out_specs=VMEM,
        compiler_params=pltpu.CompilerParams(vmem_limit_bytes=24 * MIB),
        cost_estimate=pl.CostEstimate(
            flops=2 * count * tokens * width,
            bytes_accessed=2 * (count + tokens) * width,
            transcendentals=0,
        ),
        name="dispatch",
    )(routes, stream)


def combine(stop, routes, levels, back, stream):
    tokens, width = stream.shape
    count = back.shape[0]
    return pl.pallas_call(
        functools.partial(combine_kernel, stop),
        out_shape=jax.ShapeDtypeStruct((tokens, width), stream.dtype),
        in_specs=[VMEM] * 4,
        out_specs=VMEM,
        compiler_params=pltpu.CompilerParams(vmem_limit_bytes=24 * MIB),
        cost_estimate=pl.CostEstimate(
            flops=2 * count * tokens * width,
            bytes_accessed=2 * (count + 2 * tokens) * width,
            transcendentals=0,
        ),
        name="combine",
    )(routes, levels, back, stream)


FIRST = 256


def expert_kernel(rows_ref, gain_ref, *refs):
    gate0, up0, gate1, up1, down0, down1, out_ref = refs[:7]
    gates, ups, downs, normed_ref, hidden_ref, sems = refs[7:]
    half = gate0.shape[0]
    head, tail = pl.ds(0, FIRST), pl.ds(FIRST, half - FIRST)
    blocks = [
        [(gate0.at[head], gates.at[0, head]), (up0.at[head], ups.at[0, head])],
        [(gate0.at[tail], gates.at[0, tail]), (up0.at[tail], ups.at[0, tail])],
        [(gate1, gates.at[1]), (up1, ups.at[1])],
        [(down0, downs.at[0]), (down1, downs.at[1])],
    ]
    copies = [
        [pltpu.make_async_copy(src, dst, sems.at[b, i]) for i, (src, dst) in enumerate(block)]
        for b, block in enumerate(blocks)
    ]

    def fetch(b):
        for copy in copies[b]:
            copy.start()

    def arrive(b):
        for copy in copies[b]:
            copy.wait()
        if b + DEPTH < len(copies):
            fetch(b + DEPTH)

    def hide(side, begin, end):
        gate = product_t(normed_ref[...], gates[side, begin:end])
        up = product_t(normed_ref[...], ups[side, begin:end])
        hidden_ref[side, :, begin:end] = (gate / (1.0 + jnp.exp(-gate)) * up).astype(jnp.bfloat16)

    for b in range(DEPTH):
        fetch(b)
    rowsf = rows_ref[...].astype(jnp.float32)
    variance = jnp.mean(rowsf * rowsf, axis=-1, keepdims=True)
    normed_ref[...] = (rowsf * lax.rsqrt(variance + EPS) * gain_ref[...]).astype(jnp.bfloat16)
    arrive(0)
    hide(0, 0, FIRST)
    arrive(1)
    hide(0, FIRST, half)
    arrive(2)
    hide(1, 0, half)
    arrive(3)
    for n in range(0, out_ref.shape[1], 512):
        at = slice(n, n + 512)
        out = product(hidden_ref[0], downs[0, :, at]) + product(hidden_ref[1], downs[1, :, at])
        out_ref[:, at] = out.astype(jnp.bfloat16)


def expert(rows, gain, gates, ups, downs):
    count, width = rows.shape
    half = gates[0].shape[0]
    block = pltpu.VMEM((2, half, width), jnp.bfloat16)
    return pl.pallas_call(
        expert_kernel,
        out_shape=jax.ShapeDtypeStruct((count, width), jnp.bfloat16),
        in_specs=[VMEM] * 2 + [pl.BlockSpec(memory_space=pl.ANY)] * 6,
        out_specs=VMEM,
        scratch_shapes=[block] * 3
        + [
            pltpu.VMEM((count, width), jnp.bfloat16),
            pltpu.VMEM((2, count, half), jnp.bfloat16),
            pltpu.SemaphoreType.DMA((4, 2)),
        ],
        compiler_params=pltpu.CompilerParams(vmem_limit_bytes=59 * MIB),
        cost_estimate=pl.CostEstimate(
            flops=12 * count * width * half,
            bytes_accessed=12 * half * width + 4 * count * width,
            transcendentals=2 * count * half,
        ),
        name="expert",
    )(rows, gain, gates[0], ups[0], gates[1], ups[1], *downs)


def on_device(activations, norm_gain, w_gate, w_up, w_down, routes, gate_levels):
    experts = lax.axis_size("expert") // 2
    by_token = routes[:, 0].transpose(0, 2, 1)
    levels = gate_levels[:, 0].transpose(0, 2, 1)
    stream = activations[0]
    near = (w_gate[0].T, w_up[0].T, w_down[0])
    for s in range(STOPS):
        rows = dispatch(s, by_token, stream, experts)
        if s == 0:
            rows, *near = lax.optimization_barrier((rows, *near))
            gates, ups, downs = [[w, sibling(w)] for w in near]
        rows = across_chips(rows, experts)
        back = across_chips(expert(rows, norm_gain, gates, ups, downs), experts)
        stream = passed_along(combine(s, by_token, levels, back, stream), "section", 1)
    return stream[None]


def solution(mesh):
    in_specs = (
        P("section", "expert", None),
        P("section", None),
        P("section", None, "expert"),
        P("section", None, "expert"),
        P("section", "expert", None),
        P(None, "section", "expert", None),
        P(None, "section", "expert", None),
    )
    out_specs = P("section", "expert", None)
    return jax.shard_map(
        on_device, mesh=mesh, in_specs=in_specs, out_specs=out_specs, check_vma=False
    )
```
